32 devices in a mesh: shard: 4 (over z), tensor: 4 (over y, x), section: 2 (over core).
Axes of the slice: x: 2, y: 2, z: 4, core: 2. Of those that a mesh axis runs over, the one named last changes fastest.
Arguments:
- gradient: bfloat16 [32, 512, 2048], P(('tensor', 'section'), 'shard'), may hold values from -48 to 48
- momentum: float32 [32, 512, 2048], P(('tensor', 'section'), 'shard'), may hold values from -8 to 8
- normed: bfloat16 [4096, 512], P(('shard', 'section'), 'tensor'), may hold values from -6 to 6
- ln_gain: float32 [512], P('tensor'), may hold values from 0.5 to 1.5
- ln_bias: float32 [512], P('tensor'), may hold values from -3 to 3
- ln_cotangent: bfloat16 [4096, 512], P(('shard', 'section'), 'tensor'), may hold values from -0.375 to 0.375
- router_cotangent: bfloat16 [4096, 32], P(('shard', 'section')), may hold values from -0.375 to 0.375
- first_moment: float32 [34, 512], P(None, 'tensor'), may hold values from -3 to 3
- second_moment: float32 [34, 512], P(None, 'tensor'), may hold values from 0.5 to 5
Outputs:
- next_momentum: float32 [32, 512, 2048], P(('tensor', 'section'), 'shard')
- update: float32 [32, 512, 2048], P(('tensor', 'section'), 'shard')
- next_first: float32 [34, 512], P(None, 'tensor')
- next_second: float32 [34, 512], P(None, 'tensor')
- adam_step: float32 [34, 512], P(None, 'tensor')
The draws below stay inside these ranges and needn't reach their ends.
All inputs are finite; a program needn't handle non-finite values.
Results may differ from the reference program's by a relative error of at most 0.035.
Values may be sent and summed in bfloat16 or wider, within the bound.
A program may use at most 64 MiB of HBM per device.

```python
import math
import jax
import jax.numpy as jnp
from jax import lax

D = 512
FF = 2048
EXPERTS = 32
ITERS = 5
MATS = 32
TOKENS = 4096
VECS = 34


def draw_gradient(key, part):
    keys = jax.random.split(key, 3)
    shape = (MATS, D, FF)
    base = jnp.clip(jax.random.normal(keys[0], shape, jnp.float32), -4.0, 4.0)
    row_scale = jnp.exp(jax.random.uniform(keys[1], (MATS, D, 1), jnp.float32, math.log(0.3), math.log(3.0)))
    col_scale = jnp.exp(jax.random.uniform(keys[2], (MATS, 1, FF), jnp.float32, math.log(0.3), math.log(3.0)))
    value = base * row_scale * col_scale
    return value.astype(jnp.bfloat16)


def block_levels(key, extent, pieces, low, largest):
    level, own = 1.0, jax.random.fold_in(key, 6)
    for axis_at, shards_of in pieces:
        steps = jnp.exp(jax.random.uniform(jax.random.fold_in(own, axis_at), (shards_of,), jnp.float32, low / len(pieces), largest / len(pieces)))
        level = level * jnp.repeat(steps, extent[axis_at] // shards_of).reshape([-1 if axis == axis_at else 1 for axis in range(len(extent))])
    return level


def noise(rng, shape, scale, reach, shards=(), held_as=jnp.bfloat16):
    array = scale * jax.random.normal(rng, shape, jnp.float32)
    if shards:
        array = array * block_levels(rng, shape, shards, -0.22, 0.18)
    return jnp.clip(array, -reach, reach).astype(held_as)


def setup_inputs(seed: int = 0) -> dict:
    key_list = jax.random.split(jax.random.key(seed), 10)
    return {
        "gradient": draw_gradient(jax.random.fold_in(key_list[9], 71), 0),
        "momentum": noise(key_list[1], (MATS, D, FF), 2.0, 8.0, ((0, 8), (1, 4)), jnp.float32),
        "normed": noise(key_list[2], (TOKENS, D), 1.0, 6.0, ((0, 8), (1, 4))),
        "ln_gain": jnp.clip(1.0 + 0.1 * jax.random.normal(key_list[3], (D,), jnp.float32), 0.5, 1.5),
        "ln_bias": noise(key_list[4], (D,), 0.5, 3.0, ((0, 4),), jnp.float32),
        "ln_cotangent": noise(key_list[5], (TOKENS, D), (TOKENS // 16) ** -0.5, 0.375, ((0, 8), (1, 4))),
        "router_cotangent": noise(key_list[6], (TOKENS, EXPERTS), (TOKENS // 16) ** -0.5, 0.375, ((0, 8),)),
        "first_moment": noise(key_list[7], (VECS, D), 0.5, 3.0, ((1, 4),), jnp.float32),
        "second_moment": jnp.clip(jnp.exp(math.log(5.0) - 2.3025851 * jax.random.uniform(key_list[8], (VECS, D), jnp.float32) ** block_levels(key_list[8], (VECS, D), ((1, 4),), -0.2, 0.2)), 0.5, 5.0),
    }


MUON_DECAY = 0.95
LINEAR_TERM = 3.4445
CUBIC_TERM = -4.775
QUINTIC_TERM = 2.0315
NORM_EPSILON = 1e-07
ADAM_FIRST = 0.9
ADAM_SECOND = 0.95
ADAM_EPSILON = 1e-08

def orthogonalize(matrix):
    wide = matrix.astype(jnp.float32)
    total = jnp.sqrt(jnp.sum(wide * wide))
    iterate = (wide / (total + NORM_EPSILON)).astype(jnp.bfloat16)
    for repeat in range(ITERS):
        gram = jnp.dot(iterate, iterate.T, preferred_element_type=jnp.float32)
        gram_half = gram.astype(jnp.bfloat16)
        poly = (CUBIC_TERM * gram + QUINTIC_TERM * jnp.dot(gram_half, gram_half, preferred_element_type=jnp.float32)).astype(jnp.bfloat16)
        iterate = (LINEAR_TERM * iterate.astype(jnp.float32) + jnp.dot(poly, iterate, preferred_element_type=jnp.float32)).astype(jnp.bfloat16)
    return iterate.astype(jnp.float32) * math.sqrt(FF)

def reference(gradient, momentum, normed, ln_gain, ln_bias, ln_cotangent, router_cotangent, first_moment, second_moment):
    grad_float = gradient.astype(jnp.float32)
    next_momentum = MUON_DECAY * momentum + grad_float
    nesterov = (grad_float + MUON_DECAY * next_momentum).astype(jnp.bfloat16)
    update = lax.map(orthogonalize, nesterov)
    normed_float = normed.astype(jnp.float32)
    cot_float = ln_cotangent.astype(jnp.float32)
    ln_out = (ln_gain[None, :] * normed_float + ln_bias[None, :]).astype(jnp.bfloat16)
    gain_grad = lax.optimization_barrier(jnp.sum(cot_float * normed_float, axis=0))
    bias_grad = lax.optimization_barrier(jnp.sum(cot_float, axis=0))
    router_grad = jnp.dot(router_cotangent.T, ln_out, preferred_element_type=jnp.float32)
    vec_grad = jnp.concatenate([gain_grad[None, :], bias_grad[None, :], router_grad], axis=0)
    next_first = ADAM_FIRST * first_moment + (1.0 - ADAM_FIRST) * vec_grad
    next_second = ADAM_SECOND * second_moment + (1.0 - ADAM_SECOND) * vec_grad * vec_grad
    adam_step = next_first / (jnp.sqrt(next_second) + ADAM_EPSILON)
    return (next_momentum, update, next_first, next_second, adam_step)
```

```python
import functools
import math

import jax
import jax.numpy as jnp
from jax import lax
from jax.experimental import pallas as pl
from jax.experimental.pallas import tpu as pltpu
from jax.sharding import PartitionSpec as P

D = 512
FF = 2048
EXPERTS = 32
ITERS = 5


MUON_DECAY = 0.95
LINEAR_TERM = 3.4445
CUBIC_TERM = -4.775
QUINTIC_TERM = 2.0315
NORM_EPSILON = 1e-07
ADAM_FIRST = 0.9
ADAM_SECOND = 0.95
ADAM_EPSILON = 1e-08


def keep_local(value):
    return value


def orthogonalize(blocks, join_sums, join_grams):
    squares = jnp.sum(jnp.square(blocks.astype(jnp.float32)), axis=(1, 2))
    total = jnp.sqrt(join_sums(squares))
    iterate = (blocks.astype(jnp.float32) / (total + NORM_EPSILON)[:, None, None]).astype(
        jnp.bfloat16
    )
    for repeat in range(ITERS):
        gram = join_grams(
            jnp.einsum("kij,klj->kil", iterate, iterate, preferred_element_type=jnp.float32)
        )
        gram_half = gram.astype(jnp.bfloat16)
        square_term = jnp.einsum(
            "kij,kjl->kil", gram_half, gram_half, preferred_element_type=jnp.float32
        )
        poly = (CUBIC_TERM * gram + QUINTIC_TERM * square_term).astype(jnp.bfloat16)
        product = jnp.einsum("kij,kjl->kil", poly, iterate, preferred_element_type=jnp.float32)
        iterate = (LINEAR_TERM * iterate.astype(jnp.float32) + product).astype(jnp.bfloat16)
    return iterate


def on_device(
    gradient,
    momentum,
    normed,
    ln_gain,
    ln_bias,
    ln_cotangent,
    router_cotangent,
    first_moment,
    second_moment,
):
    grad_float = gradient.astype(jnp.float32)
    next_momentum = MUON_DECAY * momentum + grad_float
    nesterov = (grad_float + MUON_DECAY * next_momentum).astype(jnp.bfloat16)
    count_all, rows_piece, cols_full = nesterov.shape
    shard_count = lax.axis_size("shard")
    normed_float = normed.astype(jnp.float32)
    cot_float = ln_cotangent.astype(jnp.float32)
    ln_out = (ln_gain[None, :] * normed_float + ln_bias[None, :]).astype(jnp.bfloat16)
    gain_local = jnp.sum(cot_float * normed_float, axis=0)
    bias_local = jnp.sum(cot_float, axis=0)
    router_local = lax.dot_general(
        router_cotangent, ln_out, (((0,), (0,)), ((), ())), preferred_element_type=jnp.float32
    )
    gain_grad, bias_grad, router_grad = lax.psum(
        (gain_local, bias_local, router_local), ("shard", "section")
    )
    vec_grad = jnp.concatenate([gain_grad[None, :], bias_grad[None, :], router_grad], axis=0)
    next_first = ADAM_FIRST * first_moment + (1.0 - ADAM_FIRST) * vec_grad
    next_second = ADAM_SECOND * second_moment + (1.0 - ADAM_SECOND) * vec_grad * vec_grad
    adam_step = next_first / (jnp.sqrt(next_second) + ADAM_EPSILON)
    slots = -(-count_all // shard_count)
    padded = jnp.pad(nesterov, ((0, slots * shard_count - count_all), (0, 0), (0, 0)))
    outgoing = padded.reshape(slots, shard_count, rows_piece, cols_full).transpose(1, 0, 2, 3)
    received = lax.all_to_all(outgoing, "shard", split_axis=0, concat_axis=0, tiled=True)
    items = received.shape[1]
    blocks = received.transpose(1, 0, 2, 3).reshape(items, shard_count * rows_piece, cols_full)
    result = orthogonalize(blocks, keep_local, keep_local)
    returned = lax.all_to_all(
        result.reshape(items, shard_count, rows_piece, cols_full).transpose(1, 0, 2, 3),
        "shard",
        split_axis=0,
        concat_axis=0,
        tiled=True,
    )
    ordered = returned.transpose(1, 0, 2, 3).reshape(slots * shard_count, rows_piece, cols_full)
    update = ordered[:count_all].astype(jnp.float32) * math.sqrt(FF)
    return (next_momentum, update, next_first, next_second, adam_step)


MESH = pl.DeviceIdType.MESH
HALF = 24
TILE = 512


def ns_kernel(
    n, grad_hbm, mom_hbm, vec_ref, back, vec_out, grad, mom, nest, mat, gram, half, poly,
    vec_peer, vec_slots, load_sem, own_sem, in_send, in_recv, out_send, out_recv,
    vs_send, vs_recv, vz_send, vz_recv, vf_send, vf_recv, gate,
):
    me = lax.axis_index("shard")
    sec = lax.axis_index("section")
    partner = {"section": 1 - sec}
    rows, cols = nest.shape[1:]
    d = n * rows
    peers = [lax.rem(me + step, n) for step in range(1, n)]
    sources = [lax.rem(me + n - step, n) for step in range(1, n)]
    order = peers + [me]

    def load(slot, k):
        return (
            pltpu.make_async_copy(grad_hbm.at[k], grad.at[slot], load_sem.at[0, slot]),
            pltpu.make_async_copy(mom_hbm.at[k], mom.at[slot], load_sem.at[1, slot]),
        )

    for slot, k in enumerate(order):
        for copy in load(slot, k):
            copy.start()

    barrier = pltpu.get_barrier_semaphore()
    for peer in peers:
        pl.semaphore_signal(barrier, inc=1, device_id={"shard": peer}, device_id_type=MESH)
    pl.semaphore_signal(barrier, inc=1, device_id=partner, device_id_type=MESH)
    pl.semaphore_wait(barrier, n)

    def remote(src, dst, send, recv, where):
        return pltpu.make_async_remote_copy(
            src_ref=src, dst_ref=dst, send_sem=send, recv_sem=recv,
            device_id=where, device_id_type=MESH,
        )

    def row_block(k):
        return mat.at[pl.ds(pl.multiple_of(k * rows, rows), rows), :]

    in_copies = [
        remote(nest.at[j], row_block(me), in_send.at[j], in_recv.at[j], {"shard": peers[j]})
        for j in range(n - 1)
    ]
    in_arrivals = [
        remote(nest.at[j], row_block(sources[j]), in_send.at[j], in_recv.at[j], {"shard": peers[j]})
        for j in range(n - 1)
    ]
    vec_swap = remote(vec_ref, vec_peer, vs_send, vs_recv, partner)
    vec_swap.start()

    for slot, k in enumerate(order):
        for copy in load(slot, k):
            copy.wait()
        wide = grad[slot].astype(jnp.float32)
        nest[slot] = (wide + MUON_DECAY * (MUON_DECAY * mom[slot] + wide)).astype(jnp.bfloat16)
        if slot < n - 1:

            @pl.when(sec == 0)
            def _():
                in_copies[slot].start()

    own = pltpu.make_async_copy(nest.at[n - 1], row_block(me), own_sem.at[0])
    own.start()

    vec_swap.wait()
    mine = pl.ds(pl.multiple_of(sec * HALF, HALF), HALF)
    vec_slots[me] = vec_ref[mine, :] + vec_peer[mine, :]
    vz = [
        remote(vec_slots.at[me], vec_slots.at[me], vz_send.at[j], vz_recv.at[j], {"shard": peers[j]})
        for j in range(n - 1)
    ]
    vz_arrivals = [
        remote(
            vec_slots.at[me], vec_slots.at[sources[j]], vz_send.at[j], vz_recv.at[j], {"shard": peers[j]}
        )
        for j in range(n - 1)
    ]
    for copy in vz:
        copy.start()

    @pl.when(sec == 1)
    def _():
        pl.semaphore_wait(gate, 1)
        for copy in in_copies:
            copy.start()

    for copy in vz:
        copy.wait_send()
    for copy in vz_arrivals:
        copy.wait_recv()
    total = vec_slots[0]
    for k in range(1, n):
        total = total + vec_slots[k]
    vec_out[mine, :] = total
    final = remote(vec_out.at[mine, :], vec_out.at[mine, :], vf_send, vf_recv, partner)
    theirs = pl.ds(pl.multiple_of((1 - sec) * HALF, HALF), HALF)
    final_arrival = remote(vec_out.at[theirs, :], vec_out.at[theirs, :], vf_send, vf_recv, partner)
    final.start()

    for copy in in_copies:
        copy.wait_send()

    @pl.when(sec == 0)
    def _():
        pl.semaphore_signal(gate, inc=1, device_id=partner, device_id_type=MESH)

    own.wait()
    for copy in in_arrivals:
        copy.wait_recv()

    nt = (((1,), (1,)), ((), ()))
    tiles = [slice(c, c + TILE) for c in range(0, cols, TILE)]

    def add_gram(i, tile):
        part = lax.dot_general(mat[:, tile], mat[:, tile], nt, preferred_element_type=jnp.float32)
        if i == 0:
            gram[...] = part
        else:
            gram[...] += part

    for i, tile in enumerate(tiles):
        add_gram(i, tile)
    on_diagonal = lax.broadcasted_iota(jnp.int32, (d, d), 0) == lax.broadcasted_iota(
        jnp.int32, (d, d), 1
    )
    trace = jnp.sum(jnp.where(on_diagonal, gram[...], 0.0))
    scale = 1.0 / (jnp.sqrt(jnp.full((1, 1), trace, jnp.float32)) + NORM_EPSILON)

    def step(repeat, scale):
        wide = gram[...] * (scale * scale)
        gram[...] = wide
        half[...] = wide.astype(jnp.bfloat16)
        square = jnp.dot(half[...], half[...], preferred_element_type=jnp.float32)
        poly[...] = ((CUBIC_TERM * gram[...] + QUINTIC_TERM * square) * scale).astype(jnp.bfloat16)
        linear = LINEAR_TERM * scale
        for i, tile in enumerate(tiles):
            now = mat[:, tile]
            product = jnp.dot(poly[...], now, preferred_element_type=jnp.float32)
            mat[:, tile] = (linear * now.astype(jnp.float32) + product).astype(jnp.bfloat16)
            add_gram(i, tile)
        return jnp.ones((1, 1), jnp.float32)

    lax.fori_loop(0, ITERS, step, scale)

    out_copies = [
        remote(row_block(peers[j]), back.at[me], out_send.at[j], out_recv.at[j], {"shard": peers[j]})
        for j in range(n - 1)
    ]
    out_arrivals = [
        remote(
            row_block(peers[j]), back.at[sources[j]], out_send.at[j], out_recv.at[j], {"shard": peers[j]}
        )
        for j in range(n - 1)
    ]
    for copy in out_copies:
        copy.start()
    keep = pltpu.make_async_copy(row_block(me), back.at[me], own_sem.at[1])
    keep.start()
    final.wait_send()
    final_arrival.wait_recv()
    keep.wait()
    for copy in out_copies:
        copy.wait_send()
    for copy in out_arrivals:
        copy.wait_recv()


def fused(gradient, momentum, vec_local):
    n, rows, cols = gradient.shape
    d = n * rows
    vmem = pl.BlockSpec(memory_space=pltpu.VMEM)
    hbm = pl.BlockSpec(memory_space=pl.ANY)
    dma = pltpu.SemaphoreType.DMA
    return pl.pallas_call(
        functools.partial(ns_kernel, n),
        out_shape=(
            jax.ShapeDtypeStruct((n, rows, cols), jnp.bfloat16),
            jax.ShapeDtypeStruct(vec_local.shape, jnp.float32),
        ),
        in_specs=[hbm, hbm, vmem],
        out_specs=(vmem, vmem),
        scratch_shapes=[
            pltpu.VMEM((n, rows, cols), jnp.bfloat16),
            pltpu.VMEM((n, rows, cols), jnp.float32),
            pltpu.VMEM((n, rows, cols), jnp.bfloat16),
            pltpu.VMEM((d, cols), jnp.bfloat16),
            pltpu.VMEM((d, d), jnp.float32),
            pltpu.VMEM((d, d), jnp.bfloat16),
            pltpu.VMEM((d, d), jnp.bfloat16),
            pltpu.VMEM(vec_local.shape, jnp.float32),
            pltpu.VMEM((n, HALF, vec_local.shape[1]), jnp.float32),
            dma((2, n)),
            dma((2,)),
            dma((n - 1,)),
            dma((n - 1,)),
            dma((n - 1,)),
            dma((n - 1,)),
            dma,
            dma,
            dma((n - 1,)),
            dma((n - 1,)),
            dma,
            dma,
            pltpu.SemaphoreType.REGULAR,
        ],
        compiler_params=pltpu.CompilerParams(
            collective_id=0, has_side_effects=True, vmem_limit_bytes=40 * 1024 * 1024
        ),
        cost_estimate=pl.CostEstimate(
            flops=2 * ITERS * d * d * (2 * cols + d), bytes_accessed=8 * d * cols, transcendentals=0
        ),
    )(gradient, momentum, vec_local)


def on_device_fused(
    gradient,
    momentum,
    normed,
    ln_gain,
    ln_bias,
    ln_cotangent,
    router_cotangent,
    first_moment,
    second_moment,
):
    next_momentum = MUON_DECAY * momentum + gradient.astype(jnp.float32)
    normed_float = normed.astype(jnp.float32)
    cot_float = ln_cotangent.astype(jnp.float32)
    ln_out = (ln_gain[None, :] * normed_float + ln_bias[None, :]).astype(jnp.bfloat16)
    gain_local = jnp.sum(cot_float * normed_float, axis=0)
    bias_local = jnp.sum(cot_float, axis=0)
    router_local = lax.dot_general(
        router_cotangent, ln_out, (((0,), (0,)), ((), ())), preferred_element_type=jnp.float32
    )
    vec_local = jnp.concatenate([gain_local[None, :], bias_local[None, :], router_local], axis=0)
    vecs = vec_local.shape[0]
    back, vec_sum = fused(gradient, momentum, jnp.pad(vec_local, ((0, 2 * HALF - vecs), (0, 0))))
    vec_grad = vec_sum[:vecs]
    next_first = ADAM_FIRST * first_moment + (1.0 - ADAM_FIRST) * vec_grad
    next_second = ADAM_SECOND * second_moment + (1.0 - ADAM_SECOND) * vec_grad * vec_grad
    adam_step = next_first / (jnp.sqrt(next_second) + ADAM_EPSILON)
    update = back.astype(jnp.float32) * math.sqrt(FF)
    return (next_momentum, update, next_first, next_second, adam_step)


def takes_kernel(shape):
    devices = shape["tensor"] * shape["section"]
    return (
        shape["section"] == 2
        and EXPERTS == devices * shape["shard"]
        and shape["shard"] > 1
        and D % (128 * shape["shard"]) == 0
    )


def solution(mesh):
    return jax.shard_map(
        on_device_fused if takes_kernel(mesh.shape) else on_device,
        mesh=mesh,
        in_specs=(
            P(("tensor", "section"), "shard", None),
            P(("tensor", "section"), "shard", None),
            P(("shard", "section"), "tensor"),
            P("tensor"),
            P("tensor"),
            P(("shard", "section"), "tensor"),
            P(("shard", "section"), None),
            P(None, "tensor"),
            P(None, "tensor"),
        ),
        out_specs=(
            P(("tensor", "section"), "shard", None),
            P(("tensor", "section"), "shard", None),
            P(None, "tensor"),
            P(None, "tensor"),
            P(None, "tensor"),
        ),
        check_vma=False,
    )
```

```python
import functools
import math

import jax
import jax.numpy as jnp
from jax import lax
from jax.experimental import pallas as pl
from jax.experimental.pallas import tpu as pltpu
from jax.sharding import PartitionSpec as P

D = 512
FF = 2048
EXPERTS = 32
ITERS = 5


MUON_DECAY = 0.95
LINEAR_TERM = 3.4445
CUBIC_TERM = -4.775
QUINTIC_TERM = 2.0315
NORM_EPSILON = 1e-07
ADAM_FIRST = 0.9
ADAM_SECOND = 0.95
ADAM_EPSILON = 1e-08


def keep_local(value):
    return value


def orthogonalize(blocks, join_sums, join_grams):
    squares = jnp.sum(jnp.square(blocks.astype(jnp.float32)), axis=(1, 2))
    total = jnp.sqrt(join_sums(squares))
    iterate = (blocks.astype(jnp.float32) / (total + NORM_EPSILON)[:, None, None]).astype(
        jnp.bfloat16
    )
    for repeat in range(ITERS):
        gram = join_grams(
            jnp.einsum("kij,klj->kil", iterate, iterate, preferred_element_type=jnp.float32)
        )
        gram_half = gram.astype(jnp.bfloat16)
        square_term = jnp.einsum(
            "kij,kjl->kil", gram_half, gram_half, preferred_element_type=jnp.float32
        )
        poly = (CUBIC_TERM * gram + QUINTIC_TERM * square_term).astype(jnp.bfloat16)
        product = jnp.einsum("kij,kjl->kil", poly, iterate, preferred_element_type=jnp.float32)
        iterate = (LINEAR_TERM * iterate.astype(jnp.float32) + product).astype(jnp.bfloat16)
    return iterate


def on_device(
    gradient,
    momentum,
    normed,
    ln_gain,
    ln_bias,
    ln_cotangent,
    router_cotangent,
    first_moment,
    second_moment,
):
    grad_float = gradient.astype(jnp.float32)
    next_momentum = MUON_DECAY * momentum + grad_float
    nesterov = (grad_float + MUON_DECAY * next_momentum).astype(jnp.bfloat16)
    count_all, rows_piece, cols_full = nesterov.shape
    shard_count = lax.axis_size("shard")
    normed_float = normed.astype(jnp.float32)
    cot_float = ln_cotangent.astype(jnp.float32)
    ln_out = (ln_gain[None, :] * normed_float + ln_bias[None, :]).astype(jnp.bfloat16)
    gain_local = jnp.sum(cot_float * normed_float, axis=0)
    bias_local = jnp.sum(cot_float, axis=0)
    router_local = lax.dot_general(
        router_cotangent, ln_out, (((0,), (0,)), ((), ())), preferred_element_type=jnp.float32
    )
    gain_grad, bias_grad, router_grad = lax.psum(
        (gain_local, bias_local, router_local), ("shard", "section")
    )
    vec_grad = jnp.concatenate([gain_grad[None, :], bias_grad[None, :], router_grad], axis=0)
    next_first = ADAM_FIRST * first_moment + (1.0 - ADAM_FIRST) * vec_grad
    next_second = ADAM_SECOND * second_moment + (1.0 - ADAM_SECOND) * vec_grad * vec_grad
    adam_step = next_first / (jnp.sqrt(next_second) + ADAM_EPSILON)
    slots = -(-count_all // shard_count)
    padded = jnp.pad(nesterov, ((0, slots * shard_count - count_all), (0, 0), (0, 0)))
    outgoing = padded.reshape(slots, shard_count, rows_piece, cols_full).transpose(1, 0, 2, 3)
    received = lax.all_to_all(outgoing, "shard", split_axis=0, concat_axis=0, tiled=True)
    items = received.shape[1]
    blocks = received.transpose(1, 0, 2, 3).reshape(items, shard_count * rows_piece, cols_full)
    result = orthogonalize(blocks, keep_local, keep_local)
    returned = lax.all_to_all(
        result.reshape(items, shard_count, rows_piece, cols_full).transpose(1, 0, 2, 3),
        "shard",
        split_axis=0,
        concat_axis=0,
        tiled=True,
    )
    ordered = returned.transpose(1, 0, 2, 3).reshape(slots * shard_count, rows_piece, cols_full)
    update = ordered[:count_all].astype(jnp.float32) * math.sqrt(FF)
    return (next_momentum, update, next_first, next_second, adam_step)


MESH = pl.DeviceIdType.MESH
HALF = 24
CHUNKS = 1
GATE = 1
TILE = 512


def flip(index, mask):
    bit = 1
    while bit <= mask:
        if mask & bit:
            index = index + bit * (1 - 2 * ((index // bit) % 2))
        bit *= 2
    return index


def ns_kernel(
    n, grad_hbm, mom_hbm, normed_hbm, cot_hbm, router_hbm, gain_ref, bias_ref, back, vec_out,
    grad, mom, nest, mat, gram, half, poly, normed, cot, router, vec_ref,
    vec_peer, vec_slots, load_sem, vec_sem, own_sem, in_send, in_recv, out_send, out_recv,
    vs_send, vs_recv, vz_send, vz_recv, vf_send, vf_recv, gate, out_gate,
):
    me = lax.axis_index("shard")
    sec = lax.axis_index("section")
    partner = {"section": 1 - sec}
    rows, cols = nest.shape[1:]
    d = n * rows
    peers = [flip(me, step) for step in range(n - 1, 0, -1)]
    sources = peers
    order = peers + [me]
    chunk = rows // CHUNKS

    def load(slot, k):
        return (
            pltpu.make_async_copy(grad_hbm.at[k], grad.at[slot], load_sem.at[0, slot]),
            pltpu.make_async_copy(mom_hbm.at[k], mom.at[slot], load_sem.at[1, slot]),
        )

    for slot, k in enumerate(order):
        for copy in load(slot, k):
            copy.start()

    vec_loads = [
        pltpu.make_async_copy(src, dst, vec_sem.at[i])
        for i, (src, dst) in enumerate(((normed_hbm, normed), (cot_hbm, cot), (router_hbm, router)))
    ]
    for copy in vec_loads:
        copy.start()

    barrier = pltpu.get_barrier_semaphore()
    for peer in peers:
        pl.semaphore_signal(barrier, inc=1, device_id={"shard": peer}, device_id_type=MESH)
    pl.semaphore_signal(barrier, inc=1, device_id=partner, device_id_type=MESH)
    pl.semaphore_wait(barrier, n)

    def remote(src, dst, send, recv, where):
        return pltpu.make_async_remote_copy(
            src_ref=src, dst_ref=dst, send_sem=send, recv_sem=recv,
            device_id=where, device_id_type=MESH,
        )

    def row_block(k):
        return mat.at[pl.ds(pl.multiple_of(k * rows, rows), rows), :]

    def in_copy(j, c, source):
        return remote(
            nest.at[j, pl.ds(c * chunk, chunk), :],
            mat.at[pl.ds(pl.multiple_of(source * rows + c * chunk, chunk), chunk), :],
            in_send.at[j, c], in_recv.at[j, c], {"shard": peers[j]},
        )

    pieces = [(j, c) for c in range(CHUNKS) for j in range(n // 2)]
    pieces += [(j, c) for c in range(CHUNKS) for j in range(n // 2, n - 1)]

    for slot, k in enumerate(order):
        for copy in load(slot, k):
            copy.wait()
        wide = grad[slot].astype(jnp.float32)
        nest[slot] = (wide + MUON_DECAY * (MUON_DECAY * mom[slot] + wide)).astype(jnp.bfloat16)
        if slot < n - 1:

            @pl.when(sec == 0)
            def _():
                for c in range(CHUNKS):
                    in_copy(slot, c, me).start()

    own = pltpu.make_async_copy(nest.at[n - 1], row_block(me), own_sem.at[0])
    own.start()

    for copy in vec_loads:
        copy.wait()
    normed_wide = normed[...].astype(jnp.float32)
    cot_wide = cot[...].astype(jnp.float32)
    ln_out = (gain_ref[...] * normed_wide + bias_ref[...]).astype(jnp.bfloat16)
    experts = router.shape[0]
    vec_ref[0:experts, :] = jnp.dot(router[...], ln_out, preferred_element_type=jnp.float32)
    gain_sum = jnp.sum(cot_wide * normed_wide, axis=0, keepdims=True)
    bias_sum = jnp.sum(cot_wide, axis=0, keepdims=True)
    rest = vec_ref.shape[0] - experts
    row = lax.broadcasted_iota(jnp.int32, (rest, cot.shape[1]), 0)
    vec_ref[experts:, :] = jnp.where(row == 0, gain_sum, jnp.where(row == 1, bias_sum, 0.0))

    vec_swap = remote(vec_ref, vec_peer, vs_send, vs_recv, partner)
    vec_swap.start()
    vec_swap.wait()
    mine = pl.ds(pl.multiple_of(sec * HALF, HALF), HALF)
    vec_slots[me] = vec_ref[mine, :] + vec_peer[mine, :]
    vz = [
        remote(vec_slots.at[me], vec_slots.at[me], vz_send.at[j], vz_recv.at[j], {"shard": peers[j]})
        for j in range(n - 1)
    ]
    vz_arrivals = [
        remote(
            vec_slots.at[me], vec_slots.at[sources[j]], vz_send.at[j], vz_recv.at[j], {"shard": peers[j]}
        )
        for j in range(n - 1)
    ]
    for copy in vz:
        copy.start()

    @pl.when(sec == 1)
    def _():
        pl.semaphore_wait(gate, 1)
        for j, c in pieces:
            in_copy(j, c, me).start()

    for copy in vz:
        copy.wait_send()
    for copy in vz_arrivals:
        copy.wait_recv()
    total = vec_slots[0]
    for k in range(1, n):
        total = total + vec_slots[k]
    vec_out[mine, :] = total
    final = remote(vec_out.at[mine, :], vec_out.at[mine, :], vf_send, vf_recv, partner)
    theirs = pl.ds(pl.multiple_of((1 - sec) * HALF, HALF), HALF)
    final_arrival = remote(vec_out.at[theirs, :], vec_out.at[theirs, :], vf_send, vf_recv, partner)
    final.start()

    for j, c in pieces[:GATE]:
        in_copy(j, c, peers[j]).wait_recv()

    @pl.when(sec == 0)
    def _():
        pl.semaphore_signal(gate, inc=1, device_id=partner, device_id_type=MESH)

    for j, c in pieces[GATE:]:
        in_copy(j, c, peers[j]).wait_recv()
    for j, c in pieces:
        in_copy(j, c, me).wait_send()
    own.wait()

    @pl.when(sec == 1)
    def _():
        pl.semaphore_signal(out_gate, inc=1, device_id=partner, device_id_type=MESH)

    nt = (((1,), (1,)), ((), ()))
    tiles = [slice(c, c + TILE) for c in range(0, cols, TILE)]

    def add_gram(i, tile):
        part = lax.dot_general(mat[:, tile], mat[:, tile], nt, preferred_element_type=jnp.float32)
        if i == 0:
            gram[...] = part
        else:
            gram[...] += part

    for i, tile in enumerate(tiles):
        add_gram(i, tile)
    on_diagonal = lax.broadcasted_iota(jnp.int32, (d, d), 0) == lax.broadcasted_iota(
        jnp.int32, (d, d), 1
    )
    trace = jnp.sum(jnp.where(on_diagonal, gram[...], 0.0))
    scale = 1.0 / (jnp.sqrt(jnp.full((1, 1), trace, jnp.float32)) + NORM_EPSILON)

    def step(repeat, scale):
        wide = gram[...] * (scale * scale)
        gram[...] = wide
        half[...] = wide.astype(jnp.bfloat16)
        square = jnp.dot(half[...], half[...], preferred_element_type=jnp.float32)
        poly[...] = ((CUBIC_TERM * gram[...] + QUINTIC_TERM * square) * scale).astype(jnp.bfloat16)
        linear = LINEAR_TERM * scale
        for i, tile in enumerate(tiles):
            now = mat[:, tile]
            product = jnp.dot(poly[...], now, preferred_element_type=jnp.float32)
            mat[:, tile] = (linear * now.astype(jnp.float32) + product).astype(jnp.bfloat16)
            add_gram(i, tile)
        return jnp.ones((1, 1), jnp.float32)

    lax.fori_loop(0, ITERS, step, scale)

    out_copies = [
        remote(row_block(peers[j]), back.at[me], out_send.at[j], out_recv.at[j], {"shard": peers[j]})
        for j in range(n - 1)
    ]
    out_arrivals = [
        remote(
            row_block(peers[j]), back.at[sources[j]], out_send.at[j], out_recv.at[j], {"shard": peers[j]}
        )
        for j in range(n - 1)
    ]

    @pl.when(sec == 0)
    def _():
        pl.semaphore_wait(out_gate, 1)

    for copy in out_copies:
        copy.start()
    keep = pltpu.make_async_copy(row_block(me), back.at[me], own_sem.at[1])
    keep.start()
    final.wait_send()
    final_arrival.wait_recv()
    keep.wait()
    for copy in out_copies:
        copy.wait_send()
    for copy in out_arrivals:
        copy.wait_recv()


def fused(gradient, momentum, normed, cotangent, router, gain, bias):
    n, rows, cols = gradient.shape
    d = n * rows
    sums = jax.ShapeDtypeStruct((2 * HALF, gain.shape[1]), jnp.float32)
    vmem = pl.BlockSpec(memory_space=pltpu.VMEM)
    hbm = pl.BlockSpec(memory_space=pltpu.HBM)
    dma = pltpu.SemaphoreType.DMA
    return pl.pallas_call(
        functools.partial(ns_kernel, n),
        out_shape=(
            jax.ShapeDtypeStruct((n, rows, cols), jnp.bfloat16),
            sums,
        ),
        in_specs=[hbm, hbm, hbm, hbm, hbm, vmem, vmem],
        out_specs=(vmem, vmem),
        scratch_shapes=[
            pltpu.VMEM((n, rows, cols), jnp.bfloat16),
            pltpu.VMEM((n, rows, cols), jnp.float32),
            pltpu.VMEM((n, rows, cols), jnp.bfloat16),
            pltpu.VMEM((d, cols), jnp.bfloat16),
            pltpu.VMEM((d, d), jnp.float32),
            pltpu.VMEM((d, d), jnp.bfloat16),
            pltpu.VMEM((d, d), jnp.bfloat16),
            pltpu.VMEM(normed.shape, jnp.bfloat16),
            pltpu.VMEM(cotangent.shape, jnp.bfloat16),
            pltpu.VMEM(router.shape, jnp.bfloat16),
            pltpu.VMEM(sums.shape, jnp.float32),
            pltpu.VMEM(sums.shape, jnp.float32),
            pltpu.VMEM((n, HALF, sums.shape[1]), jnp.float32),
            dma((2, n)),
            dma((3,)),
            dma((2,)),
            dma((n - 1, CHUNKS)),
            dma((n - 1, CHUNKS)),
            dma((n - 1,)),
            dma((n - 1,)),
            dma,
            dma,
            dma((n - 1,)),
            dma((n - 1,)),
            dma,
            dma,
            pltpu.SemaphoreType.REGULAR,
            pltpu.SemaphoreType.REGULAR,
        ],
        compiler_params=pltpu.CompilerParams(
            collective_id=0, has_side_effects=True, vmem_limit_bytes=60 * 1024 * 1024
        ),
        cost_estimate=pl.CostEstimate(
            flops=2 * ITERS * d * d * (2 * cols + d), bytes_accessed=8 * d * cols, transcendentals=0
        ),
    )(gradient, momentum, normed, cotangent, router, gain, bias)


def on_device_fused(
    gradient,
    momentum,
    normed,
    ln_gain,
    ln_bias,
    ln_cotangent,
    router_cotangent,
    first_moment,
    second_moment,
):
    next_momentum = MUON_DECAY * momentum + gradient.astype(jnp.float32)
    back, vec_sum = fused(
        gradient, momentum, normed, ln_cotangent, router_cotangent.T, ln_gain[None, :], ln_bias[None, :]
    )
    experts = router_cotangent.shape[1]
    vec_grad = jnp.concatenate([vec_sum[experts : experts + 2], vec_sum[:experts]], axis=0)
    next_first = ADAM_FIRST * first_moment + (1.0 - ADAM_FIRST) * vec_grad
    next_second = ADAM_SECOND * second_moment + (1.0 - ADAM_SECOND) * vec_grad * vec_grad
    adam_step = next_first / (jnp.sqrt(next_second) + ADAM_EPSILON)
    update = back.astype(jnp.float32) * math.sqrt(FF)
    return (next_momentum, update, next_first, next_second, adam_step)


def takes_kernel(shape):
    devices = shape["tensor"] * shape["section"]
    return (
        shape["section"] == 2
        and EXPERTS == devices * shape["shard"]
        and shape["shard"] in (2, 4)
        and D % (128 * shape["shard"]) == 0
    )


def solution(mesh):
    return jax.shard_map(
        on_device_fused if takes_kernel(mesh.shape) else on_device,
        mesh=mesh,
        in_specs=(
            P(("tensor", "section"), "shard", None),
            P(("tensor", "section"), "shard", None),
            P(("shard", "section"), "tensor"),
            P("tensor"),
            P("tensor"),
            P(("shard", "section"), "tensor"),
            P(("shard", "section"), None),
            P(None, "tensor"),
            P(None, "tensor"),
        ),
        out_specs=(
            P(("tensor", "section"), "shard", None),
            P(("tensor", "section"), "shard", None),
            P(None, "tensor"),
            P(None, "tensor"),
            P(None, "tensor"),
        ),
        check_vma=False,
    )
```

```python
import functools
import math

import jax
import jax.numpy as jnp
from jax import lax
from jax.experimental import pallas as pl
from jax.experimental.pallas import tpu as pltpu
from jax.sharding import PartitionSpec as P

D = 512
FF = 2048
EXPERTS = 32
ITERS = 5


MUON_DECAY = 0.95
LINEAR_TERM = 3.4445
CUBIC_TERM = -4.775
QUINTIC_TERM = 2.0315
NORM_EPSILON = 1e-07
ADAM_FIRST = 0.9
ADAM_SECOND = 0.95
ADAM_EPSILON = 1e-08


def keep_local(value):
    return value


def orthogonalize(blocks, join_sums, join_grams):
    squares = jnp.sum(jnp.square(blocks.astype(jnp.float32)), axis=(1, 2))
    total = jnp.sqrt(join_sums(squares))
    iterate = (blocks.astype(jnp.float32) / (total + NORM_EPSILON)[:, None, None]).astype(
        jnp.bfloat16
    )
    for repeat in range(ITERS):
        gram = join_grams(
            jnp.einsum("kij,klj->kil", iterate, iterate, preferred_element_type=jnp.float32)
        )
        gram_half = gram.astype(jnp.bfloat16)
        square_term = jnp.einsum(
            "kij,kjl->kil", gram_half, gram_half, preferred_element_type=jnp.float32
        )
        poly = (CUBIC_TERM * gram + QUINTIC_TERM * square_term).astype(jnp.bfloat16)
        product = jnp.einsum("kij,kjl->kil", poly, iterate, preferred_element_type=jnp.float32)
        iterate = (LINEAR_TERM * iterate.astype(jnp.float32) + product).astype(jnp.bfloat16)
    return iterate


def on_device(
    gradient,
    momentum,
    normed,
    ln_gain,
    ln_bias,
    ln_cotangent,
    router_cotangent,
    first_moment,
    second_moment,
):
    grad_float = gradient.astype(jnp.float32)
    next_momentum = MUON_DECAY * momentum + grad_float
    nesterov = (grad_float + MUON_DECAY * next_momentum).astype(jnp.bfloat16)
    count_all, rows_piece, cols_full = nesterov.shape
    shard_count = lax.axis_size("shard")
    normed_float = normed.astype(jnp.float32)
    cot_float = ln_cotangent.astype(jnp.float32)
    ln_out = (ln_gain[None, :] * normed_float + ln_bias[None, :]).astype(jnp.bfloat16)
    gain_local = jnp.sum(cot_float * normed_float, axis=0)
    bias_local = jnp.sum(cot_float, axis=0)
    router_local = lax.dot_general(
        router_cotangent, ln_out, (((0,), (0,)), ((), ())), preferred_element_type=jnp.float32
    )
    gain_grad, bias_grad, router_grad = lax.psum(
        (gain_local, bias_local, router_local), ("shard", "section")
    )
    vec_grad = jnp.concatenate([gain_grad[None, :], bias_grad[None, :], router_grad], axis=0)
    next_first = ADAM_FIRST * first_moment + (1.0 - ADAM_FIRST) * vec_grad
    next_second = ADAM_SECOND * second_moment + (1.0 - ADAM_SECOND) * vec_grad * vec_grad
    adam_step = next_first / (jnp.sqrt(next_second) + ADAM_EPSILON)
    slots = -(-count_all // shard_count)
    padded = jnp.pad(nesterov, ((0, slots * shard_count - count_all), (0, 0), (0, 0)))
    outgoing = padded.reshape(slots, shard_count, rows_piece, cols_full).transpose(1, 0, 2, 3)
    received = lax.all_to_all(outgoing, "shard", split_axis=0, concat_axis=0, tiled=True)
    items = received.shape[1]
    blocks = received.transpose(1, 0, 2, 3).reshape(items, shard_count * rows_piece, cols_full)
    result = orthogonalize(blocks, keep_local, keep_local)
    returned = lax.all_to_all(
        result.reshape(items, shard_count, rows_piece, cols_full).transpose(1, 0, 2, 3),
        "shard",
        split_axis=0,
        concat_axis=0,
        tiled=True,
    )
    ordered = returned.transpose(1, 0, 2, 3).reshape(slots * shard_count, rows_piece, cols_full)
    update = ordered[:count_all].astype(jnp.float32) * math.sqrt(FF)
    return (next_momentum, update, next_first, next_second, adam_step)


MESH = pl.DeviceIdType.MESH
HALF = 24
CHUNKS = 1
GATE = 1
TILE = 512


def flip(index, mask):
    bit = 1
    while bit <= mask:
        if mask & bit:
            index = index + bit * (1 - 2 * ((index // bit) % 2))
        bit *= 2
    return index


def ns_kernel(
    n, grad_hbm, mom_hbm, normed_hbm, cot_hbm, router_hbm, gain_ref, bias_ref, back, vec_out, mom,
    grad, nest, mat, gram, half, poly, normed, cot, router, vec_ref,
    vec_peer, vec_slots, load_sem, vec_sem, own_sem, in_send, in_recv, out_send, out_recv,
    vs_send, vs_recv, vz_send, vz_recv, vf_send, vf_recv, gate, out_gate,
):
    me = lax.axis_index("shard")
    sec = lax.axis_index("section")
    partner = {"section": 1 - sec}
    rows, cols = nest.shape[1:]
    d = n * rows
    peers = [flip(me, step) for step in range(n - 1, 0, -1)]
    sources = peers
    order = peers + [me]
    chunk = rows // CHUNKS

    def load(slot, k):
        return (
            pltpu.make_async_copy(grad_hbm.at[k], grad.at[slot], load_sem.at[0, slot]),
            pltpu.make_async_copy(mom_hbm.at[k], mom.at[k], load_sem.at[1, slot]),
        )

    for slot, k in enumerate(order):
        for copy in load(slot, k):
            copy.start()

    vec_loads = [
        pltpu.make_async_copy(src, dst, vec_sem.at[i])
        for i, (src, dst) in enumerate(((normed_hbm, normed), (cot_hbm, cot), (router_hbm, router)))
    ]
    for copy in vec_loads:
        copy.start()

    barrier = pltpu.get_barrier_semaphore()
    for peer in peers:
        pl.semaphore_signal(barrier, inc=1, device_id={"shard": peer}, device_id_type=MESH)
    pl.semaphore_signal(barrier, inc=1, device_id=partner, device_id_type=MESH)
    pl.semaphore_wait(barrier, n)

    def remote(src, dst, send, recv, where):
        return pltpu.make_async_remote_copy(
            src_ref=src, dst_ref=dst, send_sem=send, recv_sem=recv,
            device_id=where, device_id_type=MESH,
        )

    def row_block(k):
        return mat.at[pl.ds(pl.multiple_of(k * rows, rows), rows), :]

    def in_copy(j, c, source):
        return remote(
            nest.at[j, pl.ds(c * chunk, chunk), :],
            mat.at[pl.ds(pl.multiple_of(source * rows + c * chunk, chunk), chunk), :],
            in_send.at[j, c], in_recv.at[j, c], {"shard": peers[j]},
        )

    pieces = [(j, c) for c in range(CHUNKS) for j in range(n // 2)]
    pieces += [(j, c) for c in range(CHUNKS) for j in range(n // 2, n - 1)]

    for slot, k in enumerate(order):
        for copy in load(slot, k):
            copy.wait()
        wide = grad[slot].astype(jnp.float32)
        fresh = MUON_DECAY * mom[k] + wide
        mom[k] = fresh
        nest[slot] = (wide + MUON_DECAY * fresh).astype(jnp.bfloat16)
        if slot < n - 1:

            @pl.when(sec == 0)
            def _():
                for c in range(CHUNKS):
                    in_copy(slot, c, me).start()

    own = pltpu.make_async_copy(nest.at[n - 1], row_block(me), own_sem.at[0])
    own.start()

    for copy in vec_loads:
        copy.wait()
    normed_wide = normed[...].astype(jnp.float32)
    cot_wide = cot[...].astype(jnp.float32)
    ln_out = (gain_ref[...] * normed_wide + bias_ref[...]).astype(jnp.bfloat16)
    experts = router.shape[0]
    vec_ref[0:experts, :] = jnp.dot(router[...], ln_out, preferred_element_type=jnp.float32)
    gain_sum = jnp.sum(cot_wide * normed_wide, axis=0, keepdims=True)
    bias_sum = jnp.sum(cot_wide, axis=0, keepdims=True)
    rest = vec_ref.shape[0] - experts
    row = lax.broadcasted_iota(jnp.int32, (rest, cot.shape[1]), 0)
    vec_ref[experts:, :] = jnp.where(row == 0, gain_sum, jnp.where(row == 1, bias_sum, 0.0))

    vec_swap = remote(vec_ref, vec_peer, vs_send, vs_recv, partner)
    vec_swap.start()
    vec_swap.wait()
    mine = pl.ds(pl.multiple_of(sec * HALF, HALF), HALF)
    vec_slots[me] = vec_ref[mine, :] + vec_peer[mine, :]
    vz = [
        remote(vec_slots.at[me], vec_slots.at[me], vz_send.at[j], vz_recv.at[j], {"shard": peers[j]})
        for j in range(n - 1)
    ]
    vz_arrivals = [
        remote(
            vec_slots.at[me], vec_slots.at[sources[j]], vz_send.at[j], vz_recv.at[j], {"shard": peers[j]}
        )
        for j in range(n - 1)
    ]
    for copy in vz:
        copy.start()

    @pl.when(sec == 1)
    def _():
        pl.semaphore_wait(gate, 1)
        for j, c in pieces:
            in_copy(j, c, me).start()

    for copy in vz:
        copy.wait_send()
    for copy in vz_arrivals:
        copy.wait_recv()
    total = vec_slots[0]
    for k in range(1, n):
        total = total + vec_slots[k]
    vec_out[mine, :] = total
    final = remote(vec_out.at[mine, :], vec_out.at[mine, :], vf_send, vf_recv, partner)
    theirs = pl.ds(pl.multiple_of((1 - sec) * HALF, HALF), HALF)
    final_arrival = remote(vec_out.at[theirs, :], vec_out.at[theirs, :], vf_send, vf_recv, partner)
    final.start()

    for j, c in pieces[:GATE]:
        in_copy(j, c, peers[j]).wait_recv()

    @pl.when(sec == 0)
    def _():
        pl.semaphore_signal(gate, inc=1, device_id=partner, device_id_type=MESH)

    for j, c in pieces[GATE:]:
        in_copy(j, c, peers[j]).wait_recv()
    for j, c in pieces:
        in_copy(j, c, me).wait_send()
    own.wait()

    @pl.when(sec == 1)
    def _():
        pl.semaphore_signal(out_gate, inc=1, device_id=partner, device_id_type=MESH)

    nt = (((1,), (1,)), ((), ()))
    tiles = [slice(c, c + TILE) for c in range(0, cols, TILE)]

    def add_gram(i, tile):
        part = lax.dot_general(mat[:, tile], mat[:, tile], nt, preferred_element_type=jnp.float32)
        if i == 0:
            gram[...] = part
        else:
            gram[...] += part

    for i, tile in enumerate(tiles):
        add_gram(i, tile)
    on_diagonal = lax.broadcasted_iota(jnp.int32, (d, d), 0) == lax.broadcasted_iota(
        jnp.int32, (d, d), 1
    )
    trace = jnp.sum(jnp.where(on_diagonal, gram[...], 0.0))
    scale = 1.0 / (jnp.sqrt(jnp.full((1, 1), trace, jnp.float32)) + NORM_EPSILON)

    def step(repeat, scale):
        wide = gram[...] * (scale * scale)
        gram[...] = wide
        half[...] = wide.astype(jnp.bfloat16)
        square = jnp.dot(half[...], half[...], preferred_element_type=jnp.float32)
        poly[...] = ((CUBIC_TERM * gram[...] + QUINTIC_TERM * square) * scale).astype(jnp.bfloat16)
        linear = LINEAR_TERM * scale
        for i, tile in enumerate(tiles):
            now = mat[:, tile]
            product = jnp.dot(poly[...], now, preferred_element_type=jnp.float32)
            mat[:, tile] = (linear * now.astype(jnp.float32) + product).astype(jnp.bfloat16)
            add_gram(i, tile)
        return jnp.ones((1, 1), jnp.float32)

    lax.fori_loop(0, ITERS, step, scale)

    out_copies = [
        remote(row_block(peers[j]), back.at[me], out_send.at[j], out_recv.at[j], {"shard": peers[j]})
        for j in range(n - 1)
    ]
    out_arrivals = [
        remote(
            row_block(peers[j]), back.at[sources[j]], out_send.at[j], out_recv.at[j], {"shard": peers[j]}
        )
        for j in range(n - 1)
    ]

    @pl.when(sec == 0)
    def _():
        pl.semaphore_wait(out_gate, 1)

    for copy in out_copies:
        copy.start()
    keep = pltpu.make_async_copy(row_block(me), back.at[me], own_sem.at[1])
    keep.start()
    final.wait_send()
    final_arrival.wait_recv()
    keep.wait()
    for copy in out_copies:
        copy.wait_send()
    for copy in out_arrivals:
        copy.wait_recv()


def fused(gradient, momentum, normed, cotangent, router, gain, bias):
    n, rows, cols = gradient.shape
    d = n * rows
    sums = jax.ShapeDtypeStruct((2 * HALF, gain.shape[1]), jnp.float32)
    vmem = pl.BlockSpec(memory_space=pltpu.VMEM)
    hbm = pl.BlockSpec(memory_space=pltpu.HBM)
    dma = pltpu.SemaphoreType.DMA
    return pl.pallas_call(
        functools.partial(ns_kernel, n),
        out_shape=(
            jax.ShapeDtypeStruct((n, rows, cols), jnp.bfloat16),
            sums,
            jax.ShapeDtypeStruct((n, rows, cols), jnp.float32),
        ),
        in_specs=[hbm, hbm, hbm, hbm, hbm, vmem, vmem],
        out_specs=(vmem, vmem, vmem),
        scratch_shapes=[
            pltpu.VMEM((n, rows, cols), jnp.bfloat16),
            pltpu.VMEM((n, rows, cols), jnp.bfloat16),
            pltpu.VMEM((d, cols), jnp.bfloat16),
            pltpu.VMEM((d, d), jnp.float32),
            pltpu.VMEM((d, d), jnp.bfloat16),
            pltpu.VMEM((d, d), jnp.bfloat16),
            pltpu.VMEM(normed.shape, jnp.bfloat16),
            pltpu.VMEM(cotangent.shape, jnp.bfloat16),
            pltpu.VMEM(router.shape, jnp.bfloat16),
            pltpu.VMEM(sums.shape, jnp.float32),
            pltpu.VMEM(sums.shape, jnp.float32),
            pltpu.VMEM((n, HALF, sums.shape[1]), jnp.float32),
            dma((2, n)),
            dma((3,)),
            dma((2,)),
            dma((n - 1, CHUNKS)),
            dma((n - 1, CHUNKS)),
            dma((n - 1,)),
            dma((n - 1,)),
            dma,
            dma,
            dma((n - 1,)),
            dma((n - 1,)),
            dma,
            dma,
            pltpu.SemaphoreType.REGULAR,
            pltpu.SemaphoreType.REGULAR,
        ],
        compiler_params=pltpu.CompilerParams(
            collective_id=0, has_side_effects=True, vmem_limit_bytes=40 * 1024 * 1024
        ),
        cost_estimate=pl.CostEstimate(
            flops=2 * ITERS * d * d * (2 * cols + d), bytes_accessed=8 * d * cols, transcendentals=0
        ),
    )(gradient, momentum, normed, cotangent, router, gain, bias)


def finish_kernel(fresh, back, moment_hbm, update_hbm, wide, moment_sem, update_sem):
    n = back.shape[0]
    moments = [
        pltpu.make_async_copy(fresh.at[k], moment_hbm.at[k], moment_sem.at[k]) for k in range(n)
    ]
    updates = [
        pltpu.make_async_copy(wide.at[k], update_hbm.at[k], update_sem.at[k]) for k in range(n)
    ]
    for k in range(n):
        moments[k].start()
        wide[k] = back[k].astype(jnp.float32) * math.sqrt(FF)
        updates[k].start()
    for copy in moments + updates:
        copy.wait()


def finish(fresh, back):
    n = back.shape[0]
    result = jax.ShapeDtypeStruct(back.shape, jnp.float32)
    hbm = pl.BlockSpec(memory_space=pltpu.HBM)
    return pl.pallas_call(
        finish_kernel,
        out_shape=(result, result),
        in_specs=[pl.BlockSpec(memory_space=pltpu.VMEM)] * 2,
        out_specs=(hbm, hbm),
        scratch_shapes=[
            pltpu.VMEM(back.shape, jnp.float32),
            pltpu.SemaphoreType.DMA((n,)),
            pltpu.SemaphoreType.DMA((n,)),
        ],
        compiler_params=pltpu.CompilerParams(vmem_limit_bytes=40 * 1024 * 1024),
    )(fresh, back)


def on_device_fused(
    gradient,
    momentum,
    normed,
    ln_gain,
    ln_bias,
    ln_cotangent,
    router_cotangent,
    first_moment,
    second_moment,
):
    back, vec_sum, fresh = fused(
        gradient, momentum, normed, ln_cotangent, router_cotangent.T, ln_gain[None, :], ln_bias[None, :]
    )
    experts = router_cotangent.shape[1]
    vec_grad = jnp.concatenate([vec_sum[experts : experts + 2], vec_sum[:experts]], axis=0)
    next_first = ADAM_FIRST * first_moment + (1.0 - ADAM_FIRST) * vec_grad
    next_second = ADAM_SECOND * second_moment + (1.0 - ADAM_SECOND) * vec_grad * vec_grad
    adam_step = next_first / (jnp.sqrt(next_second) + ADAM_EPSILON)
    next_momentum, update = finish(fresh, back)
    return (next_momentum, update, next_first, next_second, adam_step)


def takes_kernel(shape):
    devices = shape["tensor"] * shape["section"]
    return (
        shape["section"] == 2
        and EXPERTS == devices * shape["shard"]
        and shape["shard"] in (2, 4)
        and D % (128 * shape["shard"]) == 0
    )


def solution(mesh):
    return jax.shard_map(
        on_device_fused if takes_kernel(mesh.shape) else on_device,
        mesh=mesh,
        in_specs=(
            P(("tensor", "section"), "shard", None),
            P(("tensor", "section"), "shard", None),
            P(("shard", "section"), "tensor"),
            P("tensor"),
            P("tensor"),
            P(("shard", "section"), "tensor"),
            P(("shard", "section"), None),
            P(None, "tensor"),
            P(None, "tensor"),
        ),
        out_specs=(
            P(("tensor", "section"), "shard", None),
            P(("tensor", "section"), "shard", None),
            P(None, "tensor"),
            P(None, "tensor"),
            P(None, "tensor"),
        ),
        check_vma=False,
    )
```
